512 devices in a mesh: dof: 32 (over z_lo, x), azi: 16 (over z_hi, y, core).
Axes of the slice: x: 4, y: 4, z: 16 (z_hi: 2, z_lo: 8; z = z_hi * 8 + z_lo), core: 2. Of those that a mesh axis runs over, the one named last changes fastest.
Arguments:
- forcing: bfloat16 [16, 256, 32768], P(None, 'azi', 'dof'), may hold values from -6 to 6
- mode_shapes: bfloat16 [32768, 2048], P('dof'), may hold values from -0.0625 to 0.0625
- inverses: bfloat16 [128, 32, 2, 64, 64], P('azi', 'dof'), may hold values from -0.5 to 0.5
- harmonic_table: int32 [128], replicated, may hold values from 0 to 127, each once
Outputs:
- displacement: bfloat16 [16, 256, 32768], P(None, 'azi', 'dof')
The draws below stay inside these ranges and needn't reach their ends.
Inputs may be any that keep to these rules, and one draw needn't show every extreme that they name: `harmonic_table`: each harmonic number appears in exactly one slot; the slots are split over azi in order.
All inputs are finite; a program needn't handle non-finite values.
Results may differ from the reference program's by a relative error of at most 0.0049.
Values may be sent and summed in bfloat16 or wider, within the bound.
A program may use at most 64 MiB of HBM per device.

```python
import math
import jax
import jax.numpy as jnp
from jax import lax

M = 2048
NAZ = 256
MB = 64
CASES = 16
DOF_DEV = 1024
NDOF = 32768
NH = 128
FAM = 32
N_DOF = 32


def with_spikes(entries, own_key, source, target, parts, factor):
    def block_of(position):
        return (jnp.arange(entries.shape[position]) // (entries.shape[position] // parts)).reshape((-1,) + (1,) * (entries.ndim - 1 - position))

    near = jax.random.permutation(own_key, parts)[block_of(target)]
    far = (block_of(target) + parts // 2) % parts
    return jnp.where((block_of(source) == near) | (block_of(source) == far), factor * entries, entries)


def block_levels(stream_key, shape, cuts, low, top_value):
    gain = 1.0
    for dim, blocks in cuts:
        draws = jax.random.uniform(jax.random.fold_in(jax.random.fold_in(stream_key, 6), dim), (blocks,), jnp.float32, low / len(cuts), top_value / len(cuts))
        gain = gain * jnp.repeat(jnp.exp(draws), shape[dim] // blocks).reshape((-1,) + (1,) * (len(shape) - 1 - dim))
    return gain


def gaussian(own_key, dims, spread, limit, cuts=(), kind=jnp.bfloat16):
    result = jax.random.normal(own_key, dims, jnp.float32) * spread
    if len(cuts) > 0:
        result = block_levels(own_key, dims, cuts, -0.22, 0.18) * result
    return jnp.clip(result, min=-limit, max=limit).astype(kind)


def gaussian_with(own_key, shape, scale, most, split, heavy, held_as=jnp.bfloat16):
    drawn = scale * jax.random.normal(own_key, shape, jnp.float32)
    if split:
        drawn = drawn * block_levels(own_key, shape, split, -0.22, 0.18)
    return jnp.clip(with_spikes(drawn, jax.random.fold_in(own_key, 3), *heavy), -most, most).astype(held_as)


def setup_inputs(seed: int = 0) -> dict:
    key_list = jax.random.split(jax.random.key(seed), 5)
    return {
        "forcing": gaussian(key_list[0], (CASES, NAZ, NDOF), 1.0, 6.0, ((1, 16), (2, 32))),
        "mode_shapes": gaussian_with(key_list[1], (NDOF, M), NDOF ** -0.5, 0.0625, ((0, 32),), (0, 1, 32, 2.75)),
        "inverses": gaussian(key_list[2], (NH, FAM, 2, MB, MB), (2 * MB) ** -0.5, 0.5, ((0, 16), (1, 32))),
        "harmonic_table": jax.random.permutation(key_list[3], NH).astype(jnp.int32),
    }


def forward_table(harmonics, samples, length):
    angles = ((samples[:, None] * harmonics[None, :]) % length).astype(jnp.float32) * (2.0 * math.pi / length)
    return jnp.stack([jnp.cos(angles), -jnp.sin(angles)], axis=2).reshape(samples.shape[0], -1)


def inverse_table(harmonics, samples, length):
    angles = ((harmonics[:, None] * samples[None, :]) % length).astype(jnp.float32) * (2.0 * math.pi / length)
    weight = jnp.where(harmonics == 0, 1.0, 2.0).astype(jnp.float32) / length
    stacked = jnp.stack([weight[:, None] * jnp.cos(angles), -weight[:, None] * jnp.sin(angles)], axis=1)
    return stacked.reshape(-1, samples.shape[0])


def contract(left, right):
    return jnp.einsum('sfik,fkcs->fics', left, right, precision=lax.Precision.HIGHEST)


def solve_modal(spectra, inverses):
    slot_count, families, _, family_size, _ = inverses.shape
    case_count = spectra.shape[1]
    pieces = spectra.reshape(families, family_size, case_count, slot_count, 2)
    real_in = pieces[..., 0]
    imag_in = pieces[..., 1]
    blocks = inverses.astype(jnp.float32)
    real_mat = blocks[:, :, 0]
    imag_mat = blocks[:, :, 1]
    real_out = contract(real_mat, real_in) - contract(imag_mat, imag_in)
    imag_out = contract(real_mat, imag_in) + contract(imag_mat, real_in)
    return jnp.stack([real_out, imag_out], axis=4).reshape(families * family_size, case_count, slot_count * 2)


def reference(forcing, mode_shapes, inverses, harmonic_table):
    case_count, sample_count, dof_count = forcing.shape
    flat = forcing.reshape(case_count * sample_count, N_DOF, DOF_DEV).transpose(1, 0, 2)
    slabs = mode_shapes.reshape(N_DOF, DOF_DEV, M)

    def add_slab(total, pair):
        shapes_slab, force_slab = pair
        partial_value = jnp.dot(shapes_slab.T, force_slab.T, preferred_element_type=jnp.float32)
        return total + partial_value, None

    start = jnp.zeros((M, case_count * sample_count), jnp.float32)
    summed, _ = lax.scan(add_slab, start, (slabs, flat))
    modal_force = summed.reshape(M, case_count, sample_count)
    samples = jnp.arange(NAZ, dtype=jnp.int32)
    spectra = jnp.einsum('mct,tj->mcj', modal_force, forward_table(harmonic_table, samples, NAZ), precision=lax.Precision.HIGHEST)
    response = solve_modal(spectra, inverses)
    modal_coords = jnp.einsum('mcj,jt->mct', response, inverse_table(harmonic_table, samples, NAZ), precision=lax.Precision.HIGHEST).astype(jnp.bfloat16)
    displaced = jnp.dot(modal_coords.reshape(M, -1).T, mode_shapes.T, preferred_element_type=jnp.float32)
    return displaced.reshape(case_count, sample_count, dof_count).astype(jnp.bfloat16)
```

```python
import functools
import math

import jax
import jax.numpy as jnp
from jax import lax
from jax.experimental import pallas as pl
from jax.experimental.pallas import tpu as pltpu
from jax.sharding import PartitionSpec as P

BF16 = jnp.bfloat16
F32 = jnp.float32
MESH = pl.DeviceIdType.MESH

DIMS = dict(Z=8, X=4, H=2, Y=4)


def kernel(
    Z, X, H, Y,
    f_hbm, s_hbm, inv_hbm, harm_hbm, out_hbm,
    f_v, s_v, inv_v, harm_v, pbuf, sendx, recvx, sendz, recvz,
    t_hi, t_lo, u_hi, u_lo, fwd, bwd, amat, xg, rg, qacc, cacc, coords, acc, out_v,
    f_sem, s_sem, i_sem, h_sem, o_sem,
    sx_sem, rx_sem, sz_sem, rz_sem, sg_sem, rg_sem, sr_sem, rr_sem,
    scz_sem, rcz_sem, scx_sem, rcx_sem,
):
    fam = inv_v.shape[2]
    slots = inv_v.shape[0]
    cases, own_t, depth = f_v.shape
    ct = cases * own_t
    azis = H * Y * 2
    length = azis * own_t
    nh = harm_v.shape[1]
    gathered = azis

    dof = lax.axis_index("dof")
    azi = lax.axis_index("azi")
    x = dof % X
    z = dof // X
    core = azi % 2
    y = (azi // 2) % Y
    h = azi // (2 * Y)

    def x_peer(r):
        return {"dof": z * X + (x + r) % X, "azi": azi}

    def z_peer(r):
        return {"dof": ((z + r) % Z) * X + x, "azi": azi}

    def y_peer(r):
        return {"dof": dof, "azi": (h * Y + (y + r) % Y) * 2 + core}

    def h_peer():
        return {"dof": dof, "azi": ((1 - h) * Y + y) * 2 + core}

    def c_peer():
        return {"dof": dof, "azi": (h * Y + y) * 2 + 1 - core}

    peers = [x_peer(r) for r in range(1, X)] + [z_peer(r) for r in range(1, Z)]
    peers += [y_peer(r) for r in range(1, Y)] + ([h_peer()] if H > 1 else []) + [c_peer()]

    barrier = pltpu.get_barrier_semaphore()
    for peer in peers:
        pl.semaphore_signal(barrier, inc=1, device_id=peer, device_id_type=MESH)

    def remote(src, dst, send, recv, peer):
        return pltpu.make_async_remote_copy(
            src_ref=src, dst_ref=dst, send_sem=send, recv_sem=recv,
            device_id=peer, device_id_type=MESH,
        )

    def f_copy():
        return pltpu.make_async_copy(f_hbm, f_v, f_sem)

    def s_copy(k):
        target = (z + 1 + k) % Z
        columns = pl.ds(pl.multiple_of(target * (X * fam), X * fam), X * fam)
        return pltpu.make_async_copy(s_hbm.at[:, columns], s_v.at[k], s_sem.at[k])

    def i_copy():
        return pltpu.make_async_copy(inv_hbm, inv_v, i_sem)

    def h_copy():
        return pltpu.make_async_copy(harm_hbm, harm_v, h_sem)

    f_copy().start()
    for k in range(Z):
        s_copy(k).start()
    h_copy().start()
    i_copy().start()
    f_copy().wait()

    def x_copy(k, r):
        rows = pl.ds(pl.multiple_of(((x + r) % X) * fam, fam), fam)
        return remote(
            sendx.at[k, rows], recvx.at[k, r - 1], sx_sem.at[k, r - 1], rx_sem.at[k, r - 1], x_peer(r)
        )

    def multiply(k):
        s_copy(k).wait()
        part = jnp.dot(f_v[...].reshape(ct, depth), s_v[k], preferred_element_type=F32)
        part = part.T
        pbuf[k] = part
        sendx[k] = part.astype(BF16)

    multiply(0)
    pl.semaphore_wait(barrier, len(peers))
    for r in range(1, X):
        x_copy(0, r).start()

    def multiply_send(k, carry):
        multiply(k)
        for r in range(1, X):
            x_copy(k, r).start()
        return carry

    lax.fori_loop(1, Z, multiply_send, 0)

    own_rows = pl.ds(pl.multiple_of(x * fam, fam), fam)

    def z_copy(k):
        return remote(sendz.at[k], recvz.at[k], sz_sem.at[k], rz_sem.at[k], z_peer(1 + k))

    def x_sum(k):
        total = pbuf[k, own_rows]
        for r in range(1, X):
            x_copy(k, r).wait_recv()
            total += recvx[k, r - 1].astype(F32)
        return total

    def x_reduce(k, carry):
        sendz[k] = x_sum(k).astype(BF16)
        z_copy(k).start()
        return carry

    lax.fori_loop(0, Z - 1, x_reduce, 0)

    h_copy().wait()
    i_copy().wait()

    harm = jnp.broadcast_to(harm_v[...].astype(F32).astype(BF16), (ct, nh))
    column = lax.broadcasted_iota(jnp.int32, (ct, nh), 0)
    lane = lax.broadcasted_iota(jnp.int32, (ct, nh), 1)
    pick = jnp.where(lane == azi * slots + column % slots, 1.0, 0.0).astype(BF16)
    lanes = (((1,), (1,)), ((), ()))
    rows_t = lax.broadcasted_iota(jnp.int32, (length, ct), 0)
    cols_t = lax.broadcasted_iota(jnp.int32, (length, ct), 1)

    def cosine(index):
        return jnp.cos(index.astype(F32) * (2.0 * math.pi / length))

    def split(value):
        high = value.astype(BF16)
        return high, (value - high.astype(F32)).astype(BF16)

    harm_rows = jnp.broadcast_to(harm_v[...].astype(F32).astype(BF16), (length, nh))
    own_h = lax.dot_general(harm_rows, pick, lanes, preferred_element_type=F32).astype(jnp.int32)
    quarter = length // 4
    part_t = (cols_t // slots) % 2
    table = cosine((own_h * rows_t + part_t * quarter) % length)
    t_hi[...], t_lo[...] = split(table)

    row_s = lax.broadcasted_iota(jnp.int32, (length, nh), 0)
    lane_s = lax.broadcasted_iota(jnp.int32, (length, nh), 1)
    pick_rows = jnp.where(
        lane_s == (row_s // (2 * slots)) * slots + row_s % slots, 1.0, 0.0
    ).astype(BF16)
    all_h = lax.dot_general(pick_rows, harm, lanes, preferred_element_type=F32).astype(jnp.int32)
    sample = azi * own_t + cols_t % own_t
    part_u = (rows_t // slots) % 2
    weight = jnp.where(all_h == 0, 1.0 / length, 2.0 / length)
    table = weight * cosine((all_h * sample + part_u * quarter) % length)
    u_hi[...], u_lo[...] = split(table)

    row_c = lax.broadcasted_iota(jnp.int32, (ct, ct), 0) // own_t
    col_c = lax.broadcasted_iota(jnp.int32, (ct, ct), 1) // own_t
    same = jnp.where(row_c == col_c, 1.0, 0.0).astype(BF16)

    def owner(slot):
        dc = slot % 2
        dy = (slot // 2) % Y
        dh = slot // (2 * Y)
        return ((h + dh) % H * Y + (y - dy + Y) % Y) * 2 + (core + dc) % 2

    def spread(ref, slot):
        rows = pl.ds(pl.multiple_of(owner(slot) * own_t, own_t), own_t)
        block = ref[rows]
        wide = jnp.broadcast_to(block[None], (cases, own_t, ct)).reshape(ct, ct)
        return wide * same

    def build_fwd(slot, carry):
        fwd[slot, 0] = spread(t_hi, slot)
        fwd[slot, 1] = spread(t_lo, slot)
        return carry

    lax.fori_loop(0, gathered, build_fwd, 0)

    total = x_sum(Z - 1)
    for k in range(Z - 1):
        z_copy(k).wait_recv()
        total += recvz[k].astype(F32)
    xg[0] = total.astype(BF16)

    def gather(buf, send, recv, consume, between):
        def slot(dh, dy, dc):
            return (dh * Y + dy) * 2 + dc

        def to_y(dh, r):
            src, dst = slot(dh, 0, 0), slot(dh, r, 0)
            return remote(buf.at[src], buf.at[dst], send.at[dst], recv.at[dst], y_peer(r))

        def to_h():
            src, dst = slot(0, 0, 0), slot(1, 0, 0)
            return remote(buf.at[src], buf.at[dst], send.at[dst], recv.at[dst], h_peer())

        def to_c(dh, dy):
            src, dst = slot(dh, dy, 0), slot(dh, dy, 1)
            return remote(buf.at[src], buf.at[dst], send.at[dst], recv.at[dst], c_peer())

        ring = [1, 3, 2] if Y == 4 else list(range(1, Y))
        if H > 1:
            to_h().start()
        for r in ring:
            to_y(0, r).start()
        to_c(0, 0).start()
        between()
        consume(slot(0, 0, 0))
        for r in ring:
            to_y(0, r).wait_recv()
            to_c(0, r).start()
        if H > 1:
            to_h().wait_recv()
            for r in ring:
                to_y(1, r).start()
            to_c(1, 0).start()
        for r in ring:
            consume(slot(0, r, 0))
        for dy in [0] + ring:
            to_c(0, dy).wait_recv()
            consume(slot(0, dy, 1))
        if H > 1:
            consume(slot(1, 0, 0))
            for r in ring:
                to_y(1, r).wait_recv()
                to_c(1, r).start()
                consume(slot(1, r, 0))
            for dy in [0] + ring:
                to_c(1, dy).wait_recv()
                consume(slot(1, dy, 1))
        for dh in range(H):
            for r in ring:
                to_y(dh, r).wait_send()
            for dy in range(Y):
                to_c(dh, dy).wait_send()
        if H > 1:
            to_h().wait_send()

    def build_bwd(slot, carry):
        bwd[slot, 0] = spread(u_hi, slot)
        bwd[slot, 1] = spread(u_lo, slot)
        return carry

    def prepare():
        for s in range(slots):
            amat[s * fam:(s + 1) * fam, 0:fam] = inv_v[s, 0]
            amat[s * fam:(s + 1) * fam, fam:2 * fam] = inv_v[s, 1]
        lax.fori_loop(0, gathered, build_bwd, 0)

    qacc[...] = jnp.zeros_like(qacc)

    def forward(slot):
        block = xg[slot]
        qacc[...] += (
            jnp.dot(block, fwd[slot, 0], preferred_element_type=F32)
            + jnp.dot(block, fwd[slot, 1], preferred_element_type=F32)
        )

    gather(xg, sg_sem, rg_sem, forward, prepare)

    q = qacc[...]
    cols = lax.broadcasted_iota(jnp.int32, (fam, ct), 1)
    turned = jnp.where(
        (cols // slots) % 2 == 0, -pltpu.roll(q, ct - slots, 1), pltpu.roll(q, slots, 1)
    )
    q_hi, q_lo = split(jnp.concatenate([q, turned], axis=0))
    solved = jnp.dot(amat[...], q_hi, preferred_element_type=F32)
    solved += jnp.dot(amat[...], q_lo, preferred_element_type=F32)
    response = jnp.zeros((fam, ct), F32)
    for s in range(slots):
        response = jnp.where(cols % slots == s, solved[s * fam:(s + 1) * fam], response)
    rg[0] = response.astype(BF16)

    cacc[...] = jnp.zeros_like(cacc)

    def backward(slot):
        block = rg[slot]
        cacc[...] += (
            jnp.dot(block, bwd[slot, 0], preferred_element_type=F32)
            + jnp.dot(block, bwd[slot, 1], preferred_element_type=F32)
        )

    gather(rg, sr_sem, rr_sem, backward, lambda: None)

    coords[0, own_rows] = cacc[...].astype(BF16)

    def c_to_z(r):
        return remote(
            coords.at[0, own_rows], coords.at[r, own_rows], scz_sem.at[r - 1], rcz_sem.at[r - 1], z_peer(r)
        )

    def c_to_x(r, q):
        return remote(
            coords.at[r, own_rows], coords.at[r, own_rows],
            scx_sem.at[r, q - 1], rcx_sem.at[r, q - 1], x_peer(q),
        )

    def c_from_x(r, q):
        rows = pl.ds(pl.multiple_of(((x - q + X) % X) * fam, fam), fam)
        return remote(
            coords.at[r, rows], coords.at[r, rows],
            scx_sem.at[r, q - 1], rcx_sem.at[r, q - 1], x_peer(q),
        )

    for q in range(1, X):
        c_to_x(0, q).start()
    for r in range(1, Z):
        c_to_z(r).start()

    acc[...] = jnp.zeros_like(acc)

    def displace(r):
        for q in range(1, X):
            c_from_x(r, q).wait_recv()
        block = coords[r].astype(F32).T.astype(BF16)
        acc[...] += lax.dot_general(block, s_v[Z - 1 - r], lanes, preferred_element_type=F32)

    def spread_displace(r, carry):
        c_to_z(r).wait_recv()
        for q in range(1, X):
            c_to_x(r, q).start()
        displace(r - 1)
        return carry

    lax.fori_loop(1, Z, spread_displace, 0)
    displace(Z - 1)

    out_v[...] = acc[...].astype(BF16).reshape(cases, own_t, depth)
    out_copy = pltpu.make_async_copy(out_v, out_hbm, o_sem)
    out_copy.start()

    def drain_x(k, carry):
        for r in range(1, X):
            x_copy(k, r).wait_send()
            c_to_x(k, r).wait_send()
        return carry

    lax.fori_loop(0, Z, drain_x, 0)
    for k in range(Z - 1):
        z_copy(k).wait_send()
        c_to_z(k + 1).wait_send()
    out_copy.wait()


def shards(dims, forcing, mode_shapes, inverses, harmonic_table):
    Z, X, H, Y = dims["Z"], dims["X"], dims["H"], dims["Y"]
    cases, own_t, depth = forcing.shape
    slots, _, _, fam, _ = inverses.shape
    ct = cases * own_t
    azis = H * Y * 2
    length = azis * own_t
    nh = harmonic_table.shape[0]
    any_space = pl.BlockSpec(memory_space=pl.ANY)
    dma = pltpu.SemaphoreType.DMA
    zs, xs = max(Z - 1, 1), max(X - 1, 1)
    return pl.pallas_call(
        functools.partial(kernel, Z, X, H, Y),
        out_shape=jax.ShapeDtypeStruct(forcing.shape, BF16),
        in_specs=[any_space] * 4,
        out_specs=any_space,
        scratch_shapes=[
            pltpu.VMEM((cases, own_t, depth), BF16),
            pltpu.VMEM((Z, depth, X * fam), BF16),
            pltpu.VMEM((slots, 2, fam, fam), BF16),
            pltpu.VMEM((1, nh), jnp.int32),
            pltpu.VMEM((Z, X * fam, ct), F32),
            pltpu.VMEM((Z, X * fam, ct), BF16),
            pltpu.VMEM((Z, xs, fam, ct), BF16),
            pltpu.VMEM((zs, fam, ct), BF16),
            pltpu.VMEM((zs, fam, ct), BF16),
            pltpu.VMEM((length, ct), BF16),
            pltpu.VMEM((length, ct), BF16),
            pltpu.VMEM((length, ct), BF16),
            pltpu.VMEM((length, ct), BF16),
            pltpu.VMEM((azis, 2, ct, ct), BF16),
            pltpu.VMEM((azis, 2, ct, ct), BF16),
            pltpu.VMEM((slots * fam, 2 * fam), BF16),
            pltpu.VMEM((azis, fam, ct), BF16),
            pltpu.VMEM((azis, fam, ct), BF16),
            pltpu.VMEM((fam, ct), F32),
            pltpu.VMEM((fam, ct), F32),
            pltpu.VMEM((Z, X * fam, ct), BF16),
            pltpu.VMEM((ct, depth), F32),
            pltpu.VMEM((cases, own_t, depth), BF16),
            dma, dma((Z,)), dma, dma, dma,
            dma((Z, xs)), dma((Z, xs)), dma((zs,)), dma((zs,)),
            dma((azis,)), dma((azis,)), dma((azis,)), dma((azis,)),
            dma((zs,)), dma((zs,)), dma((Z, xs)), dma((Z, xs)),
        ],
        compiler_params=pltpu.CompilerParams(
            collective_id=0, has_side_effects=True, vmem_limit_bytes=48 * 1024 * 1024
        ),
        name="forced_response",
    )(
        forcing,
        mode_shapes,
        inverses.reshape(slots, 2, fam, fam),
        harmonic_table.reshape(1, nh),
    )


def solution(mesh, dims=DIMS):
    in_specs = (P(None, "azi", "dof"), P("dof", None), P("azi", "dof", None, None, None), P())
    out_specs = P(None, "azi", "dof")
    return jax.shard_map(
        functools.partial(shards, dims), mesh=mesh, in_specs=in_specs, out_specs=out_specs, check_vma=False
    )
```

```python
import functools
import math

import jax
import jax.numpy as jnp
from jax import lax
from jax.experimental import pallas as pl
from jax.experimental.pallas import tpu as pltpu
from jax.sharding import PartitionSpec as P

BF16 = jnp.bfloat16
F32 = jnp.float32
MESH = pl.DeviceIdType.MESH

DIMS = dict(Z=8, X=4, H=2, Y=4)
LAG = 6


def kernel(
    Z, X, H, Y,
    f_hbm, s_hbm, inv_hbm, harm_hbm, out_hbm,
    f_v, s_v, inv_v, harm_v, pbuf, sendx, recvx, sendz, recvz, totz,
    t_hi, t_lo, u_hi, u_lo, fwd, bwd, amat, xg, rg, qacc, cacc, csend, coords, acc, out_v,
    f_sem, s_sem, i_sem, h_sem, o_sem, sa_sem, ra_sem,
    sx_sem, rx_sem, sz_sem, rz_sem, sg_sem, rg_sem, sr_sem, rr_sem,
    scz_sem, rcz_sem, scx_sem, rcx_sem,
):
    fam = inv_v.shape[2]
    slots = inv_v.shape[0]
    cases, own_t, depth = f_v.shape
    ct = cases * own_t
    half = ct // H
    group = Y * 2
    azis = H * group
    length = azis * own_t
    nh = harm_v.shape[1]
    ring = H * Z
    parts = 2 * H * slots
    own_cases = cases // H

    dof = lax.axis_index("dof")
    azi = lax.axis_index("azi")
    x = dof % X
    z = dof // X
    core = azi % 2
    y = (azi // 2) % Y
    h = azi // group
    place = h * Z + z

    def x_peer(r):
        return {"dof": z * X + (x + r) % X, "azi": azi}

    def ring_peer(r):
        there = (place + r) % ring
        return {"dof": (there % Z) * X + x, "azi": ((there // Z) * Y + y) * 2 + core}

    def y_peer(r):
        return {"dof": dof, "azi": (h * Y + (y + r) % Y) * 2 + core}

    def c_peer():
        return {"dof": dof, "azi": (h * Y + y) * 2 + 1 - core}

    peers = [ring_peer(r) for r in range(1, ring)] + [x_peer(r) for r in range(1, X)]
    peers += [y_peer(r) for r in range(1, Y)] + [c_peer()]

    barrier = pltpu.get_barrier_semaphore()
    for peer in peers:
        pl.semaphore_signal(barrier, inc=1, device_id=peer, device_id_type=MESH)

    def remote(src, dst, send, recv, peer):
        return pltpu.make_async_remote_copy(
            src_ref=src, dst_ref=dst, send_sem=send, recv_sem=recv,
            device_id=peer, device_id_type=MESH,
        )

    def offset(i):
        return jnp.where(i % 2 == 1, (i + 1) // 2, (Z - i // 2) % Z)

    def f_copy():
        return pltpu.make_async_copy(f_hbm, f_v, f_sem)

    def s_copy(o):
        target = (z + o) % Z
        columns = pl.ds(pl.multiple_of(target * (X * fam), X * fam), X * fam)
        return pltpu.make_async_copy(s_hbm.at[:, columns], s_v.at[o], s_sem.at[o])

    def i_copy():
        return pltpu.make_async_copy(inv_hbm, inv_v, i_sem)

    def h_copy():
        return pltpu.make_async_copy(harm_hbm, harm_v, h_sem)

    f_copy().start()
    for i in range(Z):
        s_copy(offset(i)).start()
    i_copy().start()
    h_copy().start()
    f_copy().wait()

    def x_copy(o, r):
        rows = pl.ds(pl.multiple_of(((x + r) % X) * fam, fam), fam)
        return remote(
            sendx.at[o, rows], recvx.at[o, r - 1], sx_sem.at[o, r - 1], rx_sem.at[o, r - 1], x_peer(r)
        )

    def multiply(o):
        s_copy(o).wait()
        part = jnp.dot(f_v[...].reshape(ct, depth), s_v[o], preferred_element_type=F32)
        part = part.T
        pbuf[o] = part
        sendx[o] = part.astype(BF16)

    multiply(0)

    i_copy().wait()
    for s in range(slots):
        amat[h, s * fam:(s + 1) * fam, 0:fam] = inv_v[s, 0]
        amat[h, s * fam:(s + 1) * fam, fam:2 * fam] = inv_v[s, 1]

    def a_copy(r):
        return remote(amat.at[h], amat.at[h], sa_sem.at[r - 1], ra_sem.at[r - 1], ring_peer(r * Z))

    def a_arrival(r):
        there = (h - r + H) % H
        return remote(amat.at[there], amat.at[there], sa_sem.at[r - 1], ra_sem.at[r - 1], ring_peer(r * Z))

    pl.semaphore_wait(barrier, len(peers))
    for r in range(1, H):
        a_copy(r).start()
    for r in range(1, X):
        x_copy(0, r).start()

    def multiply_send(i, carry):
        o = offset(i)
        multiply(o)
        for r in range(1, X):
            x_copy(o, r).start()
        return carry

    lax.fori_loop(1, Z, multiply_send, 0)

    own_rows = pl.ds(pl.multiple_of(x * fam, fam), fam)

    def z_copy(r):
        there = (place + r) % ring
        return remote(
            sendz.at[r % Z, there // Z], recvz.at[r], sz_sem.at[r], rz_sem.at[r], ring_peer(r)
        )

    def x_sum(o):
        total = pbuf[o, own_rows]
        for r in range(1, X):
            x_copy(o, r).wait_recv()
            total += recvx[o, r - 1].astype(F32)
        return total

    first = x_sum(0)
    for hh in range(H):
        piece = first[:, hh * half:(hh + 1) * half]
        sendz[0, hh] = piece.astype(BF16)
        totz[hh] = piece
    for k in range(1, H):
        z_copy(k * Z).start()
    kept = totz[h]
    totz[...] = jnp.zeros_like(totz)
    totz[h] = kept

    def x_reduce(i, carry):
        o = offset(i)
        total = x_sum(o)
        for hh in range(H):
            sendz[o, hh] = total[:, hh * half:(hh + 1) * half].astype(BF16)
        for k in range(H):
            z_copy(o + k * Z).start()
        return carry

    lax.fori_loop(1, Z, x_reduce, 0)

    h_copy().wait()
    lanes = (((1,), (1,)), ((), ()))
    table_shape = (length, ct)
    rows_t = lax.broadcasted_iota(jnp.int32, table_shape, 0)
    cols_t = lax.broadcasted_iota(jnp.int32, table_shape, 1)
    quarter = length // 4
    harm = harm_v[...].astype(F32).astype(BF16)

    def cosine(index):
        return jnp.cos((index % length).astype(F32) * (2.0 * math.pi / length))

    def split(value):
        high = value.astype(BF16)
        return high, (value - high.astype(F32)).astype(BF16)

    def slot_of(part, device):
        return (((part // slots) % H) * group + device) * slots + part % slots

    column = lax.broadcasted_iota(jnp.int32, (ct, nh), 0)
    lane = lax.broadcasted_iota(jnp.int32, (ct, nh), 1)
    pick = jnp.where(lane == slot_of(column % parts, y * 2 + core), 1.0, 0.0).astype(BF16)
    own_h = lax.dot_general(
        jnp.broadcast_to(harm, (length, nh)), pick, lanes, preferred_element_type=F32
    ).astype(jnp.int32)
    imag = (cols_t % parts) // (H * slots)
    t_hi[...], t_lo[...] = split(cosine(own_h * rows_t + imag * quarter))

    row_s = lax.broadcasted_iota(jnp.int32, (length, nh), 0)
    lane_s = lax.broadcasted_iota(jnp.int32, (length, nh), 1)
    pick_rows = jnp.where(lane_s == slot_of(row_s % parts, row_s // parts), 1.0, 0.0).astype(BF16)
    all_h = lax.dot_general(
        pick_rows, jnp.broadcast_to(harm, (ct, nh)), lanes, preferred_element_type=F32
    ).astype(jnp.int32)
    sample = ((cols_t // half) * group + y * 2 + core) * own_t + cols_t % own_t
    imag = (rows_t % parts) // (H * slots)
    weight = jnp.where(all_h == 0, 1.0 / length, 2.0 / length)
    u_hi[...], u_lo[...] = split(weight * cosine(all_h * sample + imag * quarter))

    row_c = lax.broadcasted_iota(jnp.int32, (ct, ct), 0)
    col_c = lax.broadcasted_iota(jnp.int32, (ct, ct), 1)
    same_fwd = jnp.where((row_c // own_t) % own_cases == col_c // parts, 1.0, 0.0).astype(BF16)
    same_bwd = jnp.where(row_c // parts == (col_c // own_t) % own_cases, 1.0, 0.0).astype(BF16)

    def owner(slot):
        return ((y - slot // 2 + Y) % Y) * 2 + (core + slot % 2) % 2

    def build_fwd(slot, carry):
        for n, ref in enumerate((t_hi, t_lo)):
            for hh in range(H):
                start = (hh * group + owner(slot)) * own_t
                block = ref[pl.ds(pl.multiple_of(start, own_t), own_t)]
                wide = jnp.broadcast_to(block[None], (own_cases, own_t, ct)).reshape(half, ct)
                fwd[slot, n, hh * half:(hh + 1) * half] = wide * same_fwd[hh * half:(hh + 1) * half]
        return carry

    def build_bwd(slot, carry):
        for n, ref in enumerate((u_hi, u_lo)):
            block = ref[pl.ds(pl.multiple_of(owner(slot) * parts, parts), parts)]
            wide = jnp.broadcast_to(block[None], (own_cases, parts, ct)).reshape(ct, ct)
            bwd[slot, n] = wide * same_bwd
        return carry

    lax.fori_loop(0, group, build_fwd, 0)

    def z_sum(r):
        z_copy(r).wait_recv()
        source = ((place - r + ring) % ring) // Z
        totz[source] += recvz[r].astype(F32)

    for k in range(1, H):
        z_sum(k * Z)

    def z_sums(i, carry):
        for k in range(H):
            z_sum(offset(i) + k * Z)
        return carry

    lax.fori_loop(1, Z, z_sums, 0)
    for hh in range(H):
        xg[0, :, hh * half:(hh + 1) * half] = totz[hh].astype(BF16)

    def gather(buf, send, recv, consume, between):
        def to_y(r):
            return remote(buf.at[0], buf.at[2 * r], send.at[2 * r], recv.at[2 * r], y_peer(r))

        def to_c(r):
            return remote(
                buf.at[2 * r], buf.at[2 * r + 1], send.at[2 * r + 1], recv.at[2 * r + 1], c_peer()
            )

        near = [1, 3, 2] if Y == 4 else list(range(1, Y))
        for r in near:
            to_y(r).start()
        to_c(0).start()
        between()
        consume(0)
        for r in near:
            to_y(r).wait_recv()
            to_c(r).start()
        to_c(0).wait_recv()
        consume(1)
        for r in near:
            consume(2 * r)
        for r in near:
            to_c(r).wait_recv()
            consume(2 * r + 1)
        for r in near:
            to_y(r).wait_send()
        for r in range(Y):
            to_c(r).wait_send()

    qacc[...] = jnp.zeros_like(qacc)

    def forward(slot):
        block = xg[slot]
        qacc[...] += (
            jnp.dot(block, fwd[slot, 0], preferred_element_type=F32)
            + jnp.dot(block, fwd[slot, 1], preferred_element_type=F32)
        )

    gather(xg, sg_sem, rg_sem, forward, lambda: lax.fori_loop(0, group, build_bwd, 0))

    for r in range(1, H):
        a_arrival(r).wait_recv()
    q = qacc[...]
    cols = lax.broadcasted_iota(jnp.int32, (fam, ct), 1)
    shift = H * slots
    turned = jnp.where((cols // shift) % 2 == 0, -pltpu.roll(q, ct - shift, 1), pltpu.roll(q, shift, 1))
    q_hi, q_lo = split(jnp.concatenate([q, turned], axis=0))
    response = jnp.zeros((fam, ct), F32)
    for hh in range(H):
        solved = jnp.dot(amat[hh], q_hi, preferred_element_type=F32)
        solved += jnp.dot(amat[hh], q_lo, preferred_element_type=F32)
        for s in range(slots):
            response = jnp.where(
                cols % shift == hh * slots + s, solved[s * fam:(s + 1) * fam], response
            )
    rg[0] = response.astype(BF16)

    cacc[...] = jnp.zeros_like(cacc)

    def backward(slot):
        block = rg[slot]
        cacc[...] += (
            jnp.dot(block, bwd[slot, 0], preferred_element_type=F32)
            + jnp.dot(block, bwd[slot, 1], preferred_element_type=F32)
        )

    gather(rg, sr_sem, rr_sem, backward, lambda: None)

    for hh in range(H):
        csend[hh] = cacc[:, hh * half:(hh + 1) * half].astype(BF16)
    coords[0, own_rows] = csend[h]

    def c_to_ring(r):
        there = (place + r) % ring
        return remote(
            csend.at[there // Z], coords.at[r, own_rows], scz_sem.at[r], rcz_sem.at[r], ring_peer(r)
        )

    def c_to_x(r, q):
        return remote(
            coords.at[r, own_rows], coords.at[r, own_rows],
            scx_sem.at[r, q - 1], rcx_sem.at[r, q - 1], x_peer(q),
        )

    def c_from_x(r, q):
        rows = pl.ds(pl.multiple_of(((x - q + X) % X) * fam, fam), fam)
        return remote(
            coords.at[r, rows], coords.at[r, rows],
            scx_sem.at[r, q - 1], rcx_sem.at[r, q - 1], x_peer(q),
        )

    def step(i):
        return jnp.where(i % 2 == 1, (i + 1) // 2, (ring - i // 2) % ring)

    for q in range(1, X):
        c_to_x(0, q).start()

    def send_ring(i, carry):
        c_to_ring(step(i)).start()
        return carry

    lax.fori_loop(1, ring, send_ring, 0)
    acc[...] = jnp.zeros_like(acc)

    def pass_on(i):
        r = step(i)
        c_to_ring(r).wait_recv()
        for q in range(1, X):
            c_to_x(r, q).start()

    def displace(i):
        r = step(i)
        for q in range(1, X):
            c_from_x(r, q).wait_recv()
        source = ((place - r + ring) % ring) // Z
        block = coords[r].astype(F32).T.astype(BF16)
        acc[source] += lax.dot_general(
            block, s_v[(Z - r % Z) % Z], lanes, preferred_element_type=F32
        )

    lag = min(LAG, ring)
    lax.fori_loop(1, lag, lambda i, c: (pass_on(i), c)[1], 0)
    lax.fori_loop(lag, ring, lambda i, c: (pass_on(i), displace(i - lag), c)[2], 0)
    lax.fori_loop(ring - lag, ring, lambda i, c: (displace(i), c)[1], 0)

    out_v[...] = acc[...].astype(BF16).reshape(cases, own_t, depth)
    out_copy = pltpu.make_async_copy(out_v, out_hbm, o_sem)
    out_copy.start()

    def drain_x(o, carry):
        for r in range(1, X):
            x_copy(o, r).wait_send()
        return carry

    def drain_ring(r, carry):
        z_copy(r).wait_send()
        c_to_ring(r).wait_send()
        return carry

    def drain_coords(r, carry):
        for q in range(1, X):
            c_to_x(r, q).wait_send()
        return carry

    lax.fori_loop(0, Z, drain_x, 0)
    lax.fori_loop(1, ring, drain_ring, 0)
    lax.fori_loop(0, ring, drain_coords, 0)
    for r in range(1, H):
        a_copy(r).wait_send()
    out_copy.wait()


def shards(dims, forcing, mode_shapes, inverses, harmonic_table):
    Z, X, H, Y = dims["Z"], dims["X"], dims["H"], dims["Y"]
    cases, own_t, depth = forcing.shape
    slots, _, _, fam, _ = inverses.shape
    ct = cases * own_t
    half = ct // H
    group = Y * 2
    length = H * group * own_t
    nh = harmonic_table.shape[0]
    ring = H * Z
    any_space = pl.BlockSpec(memory_space=pl.ANY)
    dma = pltpu.SemaphoreType.DMA
    xs, hs = max(X - 1, 1), max(H - 1, 1)
    return pl.pallas_call(
        functools.partial(kernel, Z, X, H, Y),
        out_shape=jax.ShapeDtypeStruct(forcing.shape, BF16),
        in_specs=[any_space] * 4,
        out_specs=any_space,
        scratch_shapes=[
            pltpu.VMEM((cases, own_t, depth), BF16),
            pltpu.VMEM((Z, depth, X * fam), BF16),
            pltpu.VMEM((slots, 2, fam, fam), BF16),
            pltpu.VMEM((1, nh), jnp.int32),
            pltpu.VMEM((Z, X * fam, ct), F32),
            pltpu.VMEM((Z, X * fam, ct), BF16),
            pltpu.VMEM((Z, xs, fam, ct), BF16),
            pltpu.VMEM((Z, H, fam, half), BF16),
            pltpu.VMEM((ring, fam, half), BF16),
            pltpu.VMEM((H, fam, half), F32),
            pltpu.VMEM((length, ct), BF16),
            pltpu.VMEM((length, ct), BF16),
            pltpu.VMEM((length, ct), BF16),
            pltpu.VMEM((length, ct), BF16),
            pltpu.VMEM((group, 2, ct, ct), BF16),
            pltpu.VMEM((group, 2, ct, ct), BF16),
            pltpu.VMEM((H, slots * fam, 2 * fam), BF16),
            pltpu.VMEM((group, fam, ct), BF16),
            pltpu.VMEM((group, fam, ct), BF16),
            pltpu.VMEM((fam, ct), F32),
            pltpu.VMEM((fam, ct), F32),
            pltpu.VMEM((H, fam, half), BF16),
            pltpu.VMEM((ring, X * fam, half), BF16),
            pltpu.VMEM((H, half, depth), F32),
            pltpu.VMEM((cases, own_t, depth), BF16),
            dma, dma((Z,)), dma, dma, dma, dma((hs,)), dma((hs,)),
            dma((Z, xs)), dma((Z, xs)), dma((ring,)), dma((ring,)),
            dma((group,)), dma((group,)), dma((group,)), dma((group,)),
            dma((ring,)), dma((ring,)), dma((ring, xs)), dma((ring, xs)),
        ],
        compiler_params=pltpu.CompilerParams(
            collective_id=0, has_side_effects=True, vmem_limit_bytes=60 * 1024 * 1024
        ),
        name="forced_response",
    )(
        forcing,
        mode_shapes,
        inverses.reshape(slots, 2, fam, fam),
        harmonic_table.reshape(1, nh),
    )


def solution(mesh, dims=DIMS):
    in_specs = (P(None, "azi", "dof"), P("dof", None), P("azi", "dof", None, None, None), P())
    out_specs = P(None, "azi", "dof")
    return jax.shard_map(
        functools.partial(shards, dims), mesh=mesh, in_specs=in_specs, out_specs=out_specs, check_vma=False
    )
```

```python
import functools
import math

import jax
import jax.numpy as jnp
from jax import lax
from jax.experimental import pallas as pl
from jax.experimental.pallas import tpu as pltpu
from jax.sharding import PartitionSpec as P

BF16 = jnp.bfloat16
F32 = jnp.float32
MESH = pl.DeviceIdType.MESH

DIMS = dict(Z=8, X=4, H=2, Y=4)
RUN = 4
INV_PIECES = 4
INV_EARLY = 2


def kernel(
    Z, X, H, Y,
    f_hbm, s_hbm, inv_hbm, harm_hbm, out_hbm,
    f_v, s_v, inv_v, harm_v, pbuf, sendx, recvx, sendz, recvz, totz,
    t_hi, t_lo, u_hi, u_lo, fwd, bwd, asend, amat, xg, rg, qacc, cacc, csend, coords, acc, out_v,
    f_sem, s_sem, i_sem, h_sem, o_sem, sa_sem, ra_sem,
    sx_sem, rx_sem, sz_sem, rz_sem, sg_sem, rg_sem, sr_sem, rr_sem,
    scz_sem, rcz_sem, scx_sem, rcx_sem,
):
    fam = inv_v.shape[2]
    slots = inv_v.shape[0]
    cases, own_t, depth = f_v.shape
    ct = cases * own_t
    half = ct // H
    group = Y * 2
    azis = H * group
    length = azis * own_t
    nh = harm_v.shape[1]
    ring = H * Z
    parts = 2 * H * slots
    own_cases = cases // H
    away = Z // 2 if H > 1 else 0

    dof = lax.axis_index("dof")
    azi = lax.axis_index("azi")
    x = dof % X
    z = dof // X
    core = azi % 2
    y = (azi // 2) % Y
    h = azi // group
    place = h * Z + z

    def x_peer(r):
        return {"dof": z * X + (x + r) % X, "azi": azi}

    def ring_peer(r):
        there = (place + r) % ring
        return {"dof": (there % Z) * X + x, "azi": ((there // Z) * Y + y) * 2 + core}

    def y_peer(r):
        return {"dof": dof, "azi": (h * Y + (y + r) % Y) * 2 + core}

    def c_peer():
        return {"dof": dof, "azi": (h * Y + y) * 2 + 1 - core}

    peers = [ring_peer(r) for r in range(1, ring)] + [x_peer(r) for r in range(1, X)]
    peers += [y_peer(r) for r in range(1, Y)] + [c_peer()]

    barrier = pltpu.get_barrier_semaphore()
    for peer in peers:
        pl.semaphore_signal(barrier, inc=1, device_id=peer, device_id_type=MESH)

    def remote(src, dst, send, recv, peer):
        return pltpu.make_async_remote_copy(
            src_ref=src, dst_ref=dst, send_sem=send, recv_sem=recv,
            device_id=peer, device_id_type=MESH,
        )

    def offset(i):
        return jnp.where(i % 2 == 1, (i + 1) // 2, (Z - i // 2) % Z)

    def f_copy():
        return pltpu.make_async_copy(f_hbm, f_v, f_sem)

    def s_copy(o):
        target = (z + o + away) % Z
        columns = pl.ds(pl.multiple_of(target * (X * fam), X * fam), X * fam)
        return pltpu.make_async_copy(s_hbm.at[:, columns], s_v.at[o], s_sem.at[o])

    def i_copy():
        return pltpu.make_async_copy(inv_hbm, inv_v, i_sem)

    def h_copy():
        return pltpu.make_async_copy(harm_hbm, harm_v, h_sem)

    f_copy().start()
    for i in range(Z):
        s_copy(offset(i)).start()
    i_copy().start()
    h_copy().start()
    f_copy().wait()

    def x_copy(o, r):
        rows = pl.ds(pl.multiple_of(((x + r) % X) * fam, fam), fam)
        return remote(
            sendx.at[o, rows], recvx.at[o, r - 1], sx_sem.at[o, r - 1], rx_sem.at[o, r - 1], x_peer(r)
        )

    def multiply(o):
        s_copy(o).wait()
        part = jnp.dot(f_v[...].reshape(ct, depth), s_v[o], preferred_element_type=F32)
        part = part.T
        pbuf[o] = part
        sendx[o] = part.astype(BF16)

    multiply(0)

    i_copy().wait()
    for s in range(slots):
        asend[s * fam:(s + 1) * fam, 0:fam] = inv_v[s, 0]
        asend[s * fam:(s + 1) * fam, fam:2 * fam] = inv_v[s, 1]
    inv_rows = slots * fam // INV_PIECES
    inv_ways = [(away + k * Z) % ring for k in range(H)]

    def a_piece(k, n, there):
        rows = slice(n * inv_rows, (n + 1) * inv_rows)
        return remote(
            asend.at[rows], amat.at[there, rows], sa_sem.at[k, n], ra_sem.at[k, n], ring_peer(inv_ways[k])
        )

    def a_copy(k, n):
        return a_piece(k, n, h)

    def a_arrival(k, n):
        return a_piece(k, n, ((place - inv_ways[k] + ring) % ring) // Z)

    if away == 0:
        amat[h] = asend[...]
    sent_inverses = [(k, n) for n in range(INV_PIECES) for k in range(H) if inv_ways[k] != 0]
    early = [(k, n) for k, n in sent_inverses if n < INV_EARLY]

    pl.semaphore_wait(barrier, len(peers))
    for k, n in early:
        a_copy(k, n).start()
    for r in range(1, X):
        x_copy(0, r).start()

    def multiply_send(i, carry):
        o = offset(i)
        multiply(o)
        for r in range(1, X):
            x_copy(o, r).start()
        return carry

    lax.fori_loop(1, Z, multiply_send, 0)

    own_rows = pl.ds(pl.multiple_of(x * fam, fam), fam)

    def z_copy(r):
        there = (place + r) % ring
        return remote(
            sendz.at[r % Z, there // Z], recvz.at[r], sz_sem.at[r], rz_sem.at[r], ring_peer(r)
        )

    def x_sum(o):
        total = pbuf[o, own_rows]
        for r in range(1, X):
            x_copy(o, r).wait_recv()
            total += recvx[o, r - 1].astype(F32)
        return total

    first = x_sum(0)
    for hh in range(H):
        piece = first[:, hh * half:(hh + 1) * half]
        sendz[0, hh] = piece.astype(BF16)
        totz[hh] = piece
    for k in range(1, H):
        z_copy(k * Z).start()
    kept = totz[h]
    totz[...] = jnp.zeros_like(totz)
    totz[h] = kept

    def x_reduce(i, carry):
        o = offset(i)
        total = x_sum(o)
        for hh in range(H):
            sendz[o, hh] = total[:, hh * half:(hh + 1) * half].astype(BF16)
        for k in range(H):
            z_copy(o + k * Z).start()
        return carry

    lax.fori_loop(1, Z, x_reduce, 0)
    for k, n in sent_inverses[len(early):]:
        a_copy(k, n).start()

    h_copy().wait()
    lanes = (((1,), (1,)), ((), ()))
    table_shape = (length, ct)
    rows_t = lax.broadcasted_iota(jnp.int32, table_shape, 0)
    cols_t = lax.broadcasted_iota(jnp.int32, table_shape, 1)
    quarter = length // 4
    harm = harm_v[...].astype(F32).astype(BF16)

    def cosine(index):
        return jnp.cos((index % length).astype(F32) * (2.0 * math.pi / length))

    def split(value):
        high = value.astype(BF16)
        return high, (value - high.astype(F32)).astype(BF16)

    def slot_of(part, device):
        return (((part // slots) % H) * group + device) * slots + part % slots

    column = lax.broadcasted_iota(jnp.int32, (ct, nh), 0)
    lane = lax.broadcasted_iota(jnp.int32, (ct, nh), 1)
    pick = jnp.where(lane == slot_of(column % parts, y * 2 + core), 1.0, 0.0).astype(BF16)
    own_h = lax.dot_general(
        jnp.broadcast_to(harm, (length, nh)), pick, lanes, preferred_element_type=F32
    ).astype(jnp.int32)
    imag = (cols_t % parts) // (H * slots)
    t_hi[...], t_lo[...] = split(cosine(own_h * rows_t + imag * quarter))

    row_s = lax.broadcasted_iota(jnp.int32, (length, nh), 0)
    lane_s = lax.broadcasted_iota(jnp.int32, (length, nh), 1)
    pick_rows = jnp.where(lane_s == slot_of(row_s % parts, row_s // parts), 1.0, 0.0).astype(BF16)
    all_h = lax.dot_general(
        pick_rows, jnp.broadcast_to(harm, (ct, nh)), lanes, preferred_element_type=F32
    ).astype(jnp.int32)
    sample = ((cols_t // half) * group + y * 2 + core) * own_t + cols_t % own_t
    imag = (rows_t % parts) // (H * slots)
    weight = jnp.where(all_h == 0, 1.0 / length, 2.0 / length)
    u_hi[...], u_lo[...] = split(weight * cosine(all_h * sample + imag * quarter))

    row_c = lax.broadcasted_iota(jnp.int32, (ct, ct), 0)
    col_c = lax.broadcasted_iota(jnp.int32, (ct, ct), 1)
    same_fwd = jnp.where((row_c // own_t) % own_cases == col_c // parts, 1.0, 0.0).astype(BF16)
    same_bwd = jnp.where(row_c // parts == (col_c // own_t) % own_cases, 1.0, 0.0).astype(BF16)

    def owner(slot):
        return ((y - slot // 2 + Y) % Y) * 2 + (core + slot % 2) % 2

    def build_fwd(slot, carry):
        for n, ref in enumerate((t_hi, t_lo)):
            for hh in range(H):
                start = (hh * group + owner(slot)) * own_t
                block = ref[pl.ds(pl.multiple_of(start, own_t), own_t)]
                wide = jnp.broadcast_to(block[None], (own_cases, own_t, ct)).reshape(half, ct)
                fwd[slot, n, hh * half:(hh + 1) * half] = wide * same_fwd[hh * half:(hh + 1) * half]
        return carry

    def build_bwd(slot, carry):
        for n, ref in enumerate((u_hi, u_lo)):
            block = ref[pl.ds(pl.multiple_of(owner(slot) * parts, parts), parts)]
            wide = jnp.broadcast_to(block[None], (own_cases, parts, ct)).reshape(ct, ct)
            bwd[slot, n] = wide * same_bwd
        return carry

    lax.fori_loop(0, group, build_fwd, 0)

    def z_sum(r):
        z_copy(r).wait_recv()
        source = ((place - r + ring) % ring) // Z
        totz[source] += recvz[r].astype(F32)

    for k in range(1, H):
        z_sum(k * Z)

    def z_sums(i, carry):
        for k in range(H):
            z_sum(offset(i) + k * Z)
        return carry

    lax.fori_loop(1, Z, z_sums, 0)
    for hh in range(H):
        xg[0, :, hh * half:(hh + 1) * half] = totz[hh].astype(BF16)

    def gather(buf, send, recv, consume, between):
        def to_y(r):
            return remote(buf.at[0], buf.at[2 * r], send.at[2 * r], recv.at[2 * r], y_peer(r))

        def to_c(r):
            return remote(
                buf.at[2 * r], buf.at[2 * r + 1], send.at[2 * r + 1], recv.at[2 * r + 1], c_peer()
            )

        near = [1, 3, 2] if Y == 4 else list(range(1, Y))
        for r in near:
            to_y(r).start()
        to_c(0).start()
        between()
        consume(0)
        for r in near:
            to_y(r).wait_recv()
            to_c(r).start()
        to_c(0).wait_recv()
        consume(1)
        for r in near:
            consume(2 * r)
        for r in near:
            to_c(r).wait_recv()
            consume(2 * r + 1)
        for r in near:
            to_y(r).wait_send()
        for r in range(Y):
            to_c(r).wait_send()

    qacc[...] = jnp.zeros_like(qacc)

    def forward(slot):
        block = xg[slot]
        qacc[...] += (
            jnp.dot(block, fwd[slot, 0], preferred_element_type=F32)
            + jnp.dot(block, fwd[slot, 1], preferred_element_type=F32)
        )

    gather(xg, sg_sem, rg_sem, forward, lambda: lax.fori_loop(0, group, build_bwd, 0))

    for k, n in sent_inverses:
        a_arrival(k, n).wait_recv()
    q = qacc[...]
    cols = lax.broadcasted_iota(jnp.int32, (fam, ct), 1)
    shift = H * slots
    turned = jnp.where((cols // shift) % 2 == 0, -pltpu.roll(q, ct - shift, 1), pltpu.roll(q, shift, 1))
    q_hi, q_lo = split(jnp.concatenate([q, turned], axis=0))
    response = jnp.zeros((fam, ct), F32)
    for hh in range(H):
        solved = jnp.dot(amat[hh], q_hi, preferred_element_type=F32)
        solved += jnp.dot(amat[hh], q_lo, preferred_element_type=F32)
        for s in range(slots):
            response = jnp.where(
                cols % shift == hh * slots + s, solved[s * fam:(s + 1) * fam], response
            )
    rg[0] = response.astype(BF16)

    cacc[...] = jnp.zeros_like(cacc)

    def backward(slot):
        block = rg[slot]
        cacc[...] += (
            jnp.dot(block, bwd[slot, 0], preferred_element_type=F32)
            + jnp.dot(block, bwd[slot, 1], preferred_element_type=F32)
        )

    gather(rg, sr_sem, rr_sem, backward, lambda: None)

    run = min(RUN, Z)
    runs = ring // run
    own_run, position = place // run, place % run
    for hh in range(H):
        csend[hh] = cacc[:, hh * half:(hh + 1) * half].astype(BF16)
    coords[0, own_rows] = csend[h]

    def place_peer(there):
        return {"dof": (there % Z) * X + x, "azi": ((there // Z) * Y + y) * 2 + core}

    def c_to_run(d):
        there = ((own_run + d) % runs) * run + position
        slot = d * run
        return remote(
            csend.at[there // Z], coords.at[slot, own_rows], scz_sem.at[slot], rcz_sem.at[slot],
            place_peer(there),
        )

    def c_in_run(d, n):
        slot = d * run + n
        return remote(
            coords.at[d * run, own_rows], coords.at[slot, own_rows], scz_sem.at[slot], rcz_sem.at[slot],
            place_peer(own_run * run + (position + n) % run),
        )

    def c_to_x(slot, q):
        return remote(
            coords.at[slot, own_rows], coords.at[slot, own_rows],
            scx_sem.at[slot, q - 1], rcx_sem.at[slot, q - 1], x_peer(q),
        )

    def c_from_x(slot, q):
        rows = pl.ds(pl.multiple_of(((x - q + X) % X) * fam, fam), fam)
        return remote(
            coords.at[slot, rows], coords.at[slot, rows],
            scx_sem.at[slot, q - 1], rcx_sem.at[slot, q - 1], x_peer(q),
        )

    def along_x(slot):
        for q in range(1, X):
            c_to_x(slot, q).start()

    def along_run(d):
        for n in range(1, run):
            c_in_run(d, n).start()

    def displace(n):
        k = n // run
        d = jnp.where(k % 2 == 1, (k + 1) // 2, (runs - k // 2) % runs)
        slot = d * run + n % run
        for q in range(1, X):
            c_from_x(slot, q).wait_recv()
        source = ((own_run - d + runs) % runs) * run + (position - n % run + run) % run
        block = coords[slot].astype(F32).T.astype(BF16)
        acc[source // Z] += lax.dot_general(
            block, s_v[(source % Z - z + Z) % Z], lanes, preferred_element_type=F32
        )

    def displace_all(low, high):
        if low < high:
            lax.fori_loop(low, high, lambda n, c: (displace(n), c)[1], 0)

    far = sorted(range(1, runs), key=lambda d: min(d, runs - d))
    for d in far[::-1]:
        c_to_run(d).start()
    along_run(0)
    along_x(0)
    acc[...] = jnp.zeros_like(acc)
    for n in range(1, run):
        c_in_run(0, n).wait_recv()
        along_x(n)
    done = 0
    for d in far:
        c_to_run(d).wait_recv()
        along_run(d)
        along_x(d * run)
        if d == far[-1]:
            displace_all(0, 1)
            done = 1
    for d in far:
        for n in range(1, run):
            c_in_run(d, n).wait_recv()
            along_x(d * run + n)
    displace_all(done, ring)

    out_v[...] = acc[...].astype(BF16).reshape(cases, own_t, depth)
    out_copy = pltpu.make_async_copy(out_v, out_hbm, o_sem)
    out_copy.start()

    def drain_x(o, carry):
        for r in range(1, X):
            x_copy(o, r).wait_send()
        return carry

    def drain_ring(r, carry):
        z_copy(r).wait_send()
        return carry

    def drain_coords(r, carry):
        for q in range(1, X):
            c_to_x(r, q).wait_send()
        return carry

    lax.fori_loop(0, Z, drain_x, 0)
    lax.fori_loop(1, ring, drain_ring, 0)
    lax.fori_loop(0, ring, drain_coords, 0)
    for d in far:
        c_to_run(d).wait_send()
    for d in range(runs):
        for n in range(1, run):
            c_in_run(d, n).wait_send()
    for k, n in sent_inverses:
        a_copy(k, n).wait_send()
    out_copy.wait()


def shards(dims, forcing, mode_shapes, inverses, harmonic_table):
    Z, X, H, Y = dims["Z"], dims["X"], dims["H"], dims["Y"]
    cases, own_t, depth = forcing.shape
    slots, _, _, fam, _ = inverses.shape
    ct = cases * own_t
    half = ct // H
    group = Y * 2
    length = H * group * own_t
    nh = harmonic_table.shape[0]
    ring = H * Z
    any_space = pl.BlockSpec(memory_space=pl.ANY)
    dma = pltpu.SemaphoreType.DMA
    xs = max(X - 1, 1)
    return pl.pallas_call(
        functools.partial(kernel, Z, X, H, Y),
        out_shape=jax.ShapeDtypeStruct(forcing.shape, BF16),
        in_specs=[any_space] * 4,
        out_specs=any_space,
        scratch_shapes=[
            pltpu.VMEM((cases, own_t, depth), BF16),
            pltpu.VMEM((Z, depth, X * fam), BF16),
            pltpu.VMEM((slots, 2, fam, fam), BF16),
            pltpu.VMEM((1, nh), jnp.int32),
            pltpu.VMEM((Z, X * fam, ct), F32),
            pltpu.VMEM((Z, X * fam, ct), BF16),
            pltpu.VMEM((Z, xs, fam, ct), BF16),
            pltpu.VMEM((Z, H, fam, half), BF16),
            pltpu.VMEM((ring, fam, half), BF16),
            pltpu.VMEM((H, fam, half), F32),
            pltpu.VMEM((length, ct), BF16),
            pltpu.VMEM((length, ct), BF16),
            pltpu.VMEM((length, ct), BF16),
            pltpu.VMEM((length, ct), BF16),
            pltpu.VMEM((group, 2, ct, ct), BF16),
            pltpu.VMEM((group, 2, ct, ct), BF16),
            pltpu.VMEM((slots * fam, 2 * fam), BF16),
            pltpu.VMEM((H, slots * fam, 2 * fam), BF16),
            pltpu.VMEM((group, fam, ct), BF16),
            pltpu.VMEM((group, fam, ct), BF16),
            pltpu.VMEM((fam, ct), F32),
            pltpu.VMEM((fam, ct), F32),
            pltpu.VMEM((H, fam, half), BF16),
            pltpu.VMEM((ring, X * fam, half), BF16),
            pltpu.VMEM((H, half, depth), F32),
            pltpu.VMEM((cases, own_t, depth), BF16),
            dma, dma((Z,)), dma, dma, dma, dma((H, INV_PIECES)), dma((H, INV_PIECES)),
            dma((Z, xs)), dma((Z, xs)), dma((ring,)), dma((ring,)),
            dma((group,)), dma((group,)), dma((group,)), dma((group,)),
            dma((ring,)), dma((ring,)), dma((ring, xs)), dma((ring, xs)),
        ],
        compiler_params=pltpu.CompilerParams(
            collective_id=0, has_side_effects=True, vmem_limit_bytes=60 * 1024 * 1024
        ),
        name="forced_response",
    )(
        forcing,
        mode_shapes,
        inverses.reshape(slots, 2, fam, fam),
        harmonic_table.reshape(1, nh),
    )


def solution(mesh, dims=DIMS):
    in_specs = (P(None, "azi", "dof"), P("dof", None), P("azi", "dof", None, None, None), P())
    out_specs = P(None, "azi", "dof")
    return jax.shard_map(
        functools.partial(shards, dims), mesh=mesh, in_specs=in_specs, out_specs=out_specs, check_vma=False
    )
```

```python
import functools
import math

import jax
import jax.numpy as jnp
from jax import lax
from jax.experimental import pallas as pl
from jax.experimental.pallas import tpu as pltpu
from jax.sharding import PartitionSpec as P

BF16 = jnp.bfloat16
F32 = jnp.float32
MESH = pl.DeviceIdType.MESH

DIMS = dict(Z=8, X=4, H=2, Y=4)
RUN = 4
INV_PIECES = 4
INV_EARLY = 2


def kernel(
    Z, X, H, Y,
    f_hbm, s_hbm, inv_hbm, harm_hbm, out_hbm,
    f_v, s_v, inv_v, harm_v, pbuf, sendx, recvx, sendz, recvz, totz,
    t_hi, t_lo, u_hi, u_lo, fwd, bwd, asend, amat, xg, rg, qacc, cacc, csend, coords, acc, out_v,
    f_sem, s_sem, i_sem, h_sem, o_sem, sa_sem, ra_sem,
    sx_sem, rx_sem, sz_sem, rz_sem, sg_sem, rg_sem, sr_sem, rr_sem,
    scz_sem, rcz_sem, scx_sem, rcx_sem,
):
    fam = inv_v.shape[2]
    slots = inv_v.shape[0]
    cases, own_t, depth = f_v.shape
    ct = cases * own_t
    half = ct // H
    group = Y * 2
    azis = H * group
    length = azis * own_t
    nh = harm_v.shape[1]
    ring = H * Z
    parts = 2 * H * slots
    own_cases = cases // H
    away = Z // 2 if H > 1 else 0

    dof = lax.axis_index("dof")
    azi = lax.axis_index("azi")
    x = dof % X
    z = dof // X
    core = azi % 2
    y = (azi // 2) % Y
    h = azi // group
    place = h * Z + z

    far_x = sorted(range(1, X), key=lambda r: -min(r, X - r))

    def x_peer(r):
        return {"dof": z * X + (x + r) % X, "azi": azi}

    def ring_peer(r):
        there = (place + r) % ring
        return {"dof": (there % Z) * X + x, "azi": ((there // Z) * Y + y) * 2 + core}

    def y_peer(r):
        return {"dof": dof, "azi": (h * Y + (y + r) % Y) * 2 + core}

    def c_peer():
        return {"dof": dof, "azi": (h * Y + y) * 2 + 1 - core}

    peers = [ring_peer(r) for r in range(1, ring)] + [x_peer(r) for r in range(1, X)]
    peers += [y_peer(r) for r in range(1, Y)] + [c_peer()]

    barrier = pltpu.get_barrier_semaphore()
    for peer in peers:
        pl.semaphore_signal(barrier, inc=1, device_id=peer, device_id_type=MESH)

    def remote(src, dst, send, recv, peer):
        return pltpu.make_async_remote_copy(
            src_ref=src, dst_ref=dst, send_sem=send, recv_sem=recv,
            device_id=peer, device_id_type=MESH,
        )

    def offset(i):
        return jnp.where(i % 2 == 1, (i + 1) // 2, (Z - i // 2) % Z)

    def f_copy():
        return pltpu.make_async_copy(f_hbm, f_v, f_sem)

    def s_copy(o):
        target = (z + o + away) % Z
        columns = pl.ds(pl.multiple_of(target * (X * fam), X * fam), X * fam)
        return pltpu.make_async_copy(s_hbm.at[:, columns], s_v.at[o], s_sem.at[o])

    def i_copy():
        return pltpu.make_async_copy(inv_hbm, inv_v, i_sem)

    def h_copy():
        return pltpu.make_async_copy(harm_hbm, harm_v, h_sem)

    f_copy().start()
    for i in range(Z):
        s_copy(offset(i)).start()
    i_copy().start()
    h_copy().start()
    f_copy().wait()

    def x_copy(o, r):
        rows = pl.ds(pl.multiple_of(((x + r) % X) * fam, fam), fam)
        return remote(
            sendx.at[o, rows], recvx.at[o, r - 1], sx_sem.at[o, r - 1], rx_sem.at[o, r - 1], x_peer(r)
        )

    def multiply(o):
        s_copy(o).wait()
        part = jnp.dot(f_v[...].reshape(ct, depth), s_v[o], preferred_element_type=F32)
        part = part.T
        pbuf[o] = part
        sendx[o] = part.astype(BF16)

    multiply(0)

    i_copy().wait()
    for s in range(slots):
        asend[s * fam:(s + 1) * fam, 0:fam] = inv_v[s, 0]
        asend[s * fam:(s + 1) * fam, fam:2 * fam] = inv_v[s, 1]
    inv_rows = slots * fam // INV_PIECES
    inv_ways = [(away + k * Z) % ring for k in range(H)]

    def a_piece(k, n, there):
        rows = slice(n * inv_rows, (n + 1) * inv_rows)
        return remote(
            asend.at[rows], amat.at[there, rows], sa_sem.at[k, n], ra_sem.at[k, n], ring_peer(inv_ways[k])
        )

    def a_copy(k, n):
        return a_piece(k, n, h)

    def a_arrival(k, n):
        return a_piece(k, n, ((place - inv_ways[k] + ring) % ring) // Z)

    if away == 0:
        amat[h] = asend[...]
    sent_inverses = [(k, n) for n in range(INV_PIECES) for k in range(H) if inv_ways[k] != 0]
    early = [(k, n) for k, n in sent_inverses if n < INV_EARLY]

    pl.semaphore_wait(barrier, len(peers))
    for k, n in early:
        a_copy(k, n).start()
    for r in range(1, X):
        x_copy(0, r).start()

    def multiply_send(i, carry):
        o = offset(i)
        multiply(o)
        for r in far_x:
            x_copy(o, r).start()
        return carry

    lax.fori_loop(1, Z, multiply_send, 0)

    own_rows = pl.ds(pl.multiple_of(x * fam, fam), fam)

    def z_copy(r):
        there = (place + r) % ring
        return remote(
            sendz.at[r % Z, there // Z], recvz.at[r], sz_sem.at[r], rz_sem.at[r], ring_peer(r)
        )

    def x_sum(o):
        total = pbuf[o, own_rows]
        for r in range(1, X):
            x_copy(o, r).wait_recv()
            total += recvx[o, r - 1].astype(F32)
        return total

    first = x_sum(0)
    for hh in range(H):
        piece = first[:, hh * half:(hh + 1) * half]
        sendz[0, hh] = piece.astype(BF16)
        totz[hh] = piece
    for k in range(1, H):
        z_copy(k * Z).start()
    kept = totz[h]
    totz[...] = jnp.zeros_like(totz)
    totz[h] = kept

    def x_reduce(i, carry):
        o = offset(i)
        total = x_sum(o)
        for hh in range(H):
            sendz[o, hh] = total[:, hh * half:(hh + 1) * half].astype(BF16)
        for k in range(H):
            z_copy(o + k * Z).start()
        return carry

    lax.fori_loop(1, Z, x_reduce, 0)
    for k, n in sent_inverses[len(early):]:
        a_copy(k, n).start()

    h_copy().wait()
    lanes = (((1,), (1,)), ((), ()))
    table_shape = (length, ct)
    rows_t = lax.broadcasted_iota(jnp.int32, table_shape, 0)
    cols_t = lax.broadcasted_iota(jnp.int32, table_shape, 1)
    quarter = length // 4
    harm = harm_v[...].astype(F32).astype(BF16)

    def cosine(index):
        return jnp.cos((index % length).astype(F32) * (2.0 * math.pi / length))

    def split(value):
        high = value.astype(BF16)
        return high, (value - high.astype(F32)).astype(BF16)

    def slot_of(part, device):
        return (((part // slots) % H) * group + device) * slots + part % slots

    column = lax.broadcasted_iota(jnp.int32, (ct, nh), 0)
    lane = lax.broadcasted_iota(jnp.int32, (ct, nh), 1)
    pick = jnp.where(lane == slot_of(column % parts, y * 2 + core), 1.0, 0.0).astype(BF16)
    own_h = lax.dot_general(
        jnp.broadcast_to(harm, (length, nh)), pick, lanes, preferred_element_type=F32
    ).astype(jnp.int32)
    imag = (cols_t % parts) // (H * slots)
    t_hi[...], t_lo[...] = split(cosine(own_h * rows_t + imag * quarter))

    row_s = lax.broadcasted_iota(jnp.int32, (length, nh), 0)
    lane_s = lax.broadcasted_iota(jnp.int32, (length, nh), 1)
    pick_rows = jnp.where(lane_s == slot_of(row_s % parts, row_s // parts), 1.0, 0.0).astype(BF16)
    all_h = lax.dot_general(
        pick_rows, jnp.broadcast_to(harm, (ct, nh)), lanes, preferred_element_type=F32
    ).astype(jnp.int32)
    sample = ((cols_t // half) * group + y * 2 + core) * own_t + cols_t % own_t
    imag = (rows_t % parts) // (H * slots)
    weight = jnp.where(all_h == 0, 1.0 / length, 2.0 / length)
    u_hi[...], u_lo[...] = split(weight * cosine(all_h * sample + imag * quarter))

    row_c = lax.broadcasted_iota(jnp.int32, (ct, ct), 0)
    col_c = lax.broadcasted_iota(jnp.int32, (ct, ct), 1)
    same_fwd = jnp.where((row_c // own_t) % own_cases == col_c // parts, 1.0, 0.0).astype(BF16)
    same_bwd = jnp.where(row_c // parts == (col_c // own_t) % own_cases, 1.0, 0.0).astype(BF16)

    def owner(slot):
        return ((y - slot // 2 + Y) % Y) * 2 + (core + slot % 2) % 2

    def build_fwd(slot, carry):
        for n, ref in enumerate((t_hi, t_lo)):
            for hh in range(H):
                start = (hh * group + owner(slot)) * own_t
                block = ref[pl.ds(pl.multiple_of(start, own_t), own_t)]
                wide = jnp.broadcast_to(block[None], (own_cases, own_t, ct)).reshape(half, ct)
                fwd[slot, n, hh * half:(hh + 1) * half] = wide * same_fwd[hh * half:(hh + 1) * half]
        return carry

    def build_bwd(slot, carry):
        for n, ref in enumerate((u_hi, u_lo)):
            block = ref[pl.ds(pl.multiple_of(owner(slot) * parts, parts), parts)]
            wide = jnp.broadcast_to(block[None], (own_cases, parts, ct)).reshape(ct, ct)
            bwd[slot, n] = wide * same_bwd
        return carry

    lax.fori_loop(0, group, build_fwd, 0)

    def z_sum(r):
        z_copy(r).wait_recv()
        source = ((place - r + ring) % ring) // Z
        totz[source] += recvz[r].astype(F32)

    for k in range(1, H):
        z_sum(k * Z)

    def z_sums(i, carry):
        for k in range(H):
            z_sum(offset(i) + k * Z)
        return carry

    lax.fori_loop(1, Z, z_sums, 0)
    for hh in range(H):
        xg[0, :, hh * half:(hh + 1) * half] = totz[hh].astype(BF16)

    def gather(buf, send, recv, consume, between):
        def to_y(r):
            return remote(buf.at[0], buf.at[2 * r], send.at[2 * r], recv.at[2 * r], y_peer(r))

        def to_c(r):
            return remote(
                buf.at[2 * r], buf.at[2 * r + 1], send.at[2 * r + 1], recv.at[2 * r + 1], c_peer()
            )

        near = [1, 3, 2] if Y == 4 else list(range(1, Y))
        for r in near:
            to_y(r).start()
        to_c(0).start()
        between()
        consume(0)
        for r in near:
            to_y(r).wait_recv()
            to_c(r).start()
        to_c(0).wait_recv()
        consume(1)
        for r in near:
            consume(2 * r)
        for r in near:
            to_c(r).wait_recv()
            consume(2 * r + 1)
        for r in near:
            to_y(r).wait_send()
        for r in range(Y):
            to_c(r).wait_send()

    qacc[...] = jnp.zeros_like(qacc)

    def forward(slot):
        block = xg[slot]
        qacc[...] += (
            jnp.dot(block, fwd[slot, 0], preferred_element_type=F32)
            + jnp.dot(block, fwd[slot, 1], preferred_element_type=F32)
        )

    gather(xg, sg_sem, rg_sem, forward, lambda: lax.fori_loop(0, group, build_bwd, 0))

    q = qacc[...]
    cols = lax.broadcasted_iota(jnp.int32, (fam, ct), 1)
    shift = H * slots
    turned = jnp.where((cols // shift) % 2 == 0, -pltpu.roll(q, ct - shift, 1), pltpu.roll(q, shift, 1))
    q_hi, q_lo = split(jnp.concatenate([q, turned], axis=0))
    response = jnp.zeros((fam, ct), F32)
    piece_slots = slots // INV_PIECES
    for n in range(INV_PIECES):
        for k, piece in sent_inverses:
            if piece == n:
                a_arrival(k, piece).wait_recv()
        for hh in range(H):
            block = amat[hh, n * inv_rows:(n + 1) * inv_rows]
            solved = jnp.dot(block, q_hi, preferred_element_type=F32)
            solved += jnp.dot(block, q_lo, preferred_element_type=F32)
            for s in range(piece_slots):
                response = jnp.where(
                    cols % shift == hh * slots + n * piece_slots + s,
                    solved[s * fam:(s + 1) * fam], response,
                )
    rg[0] = response.astype(BF16)

    cacc[...] = jnp.zeros_like(cacc)

    def backward(slot):
        block = rg[slot]
        cacc[...] += (
            jnp.dot(block, bwd[slot, 0], preferred_element_type=F32)
            + jnp.dot(block, bwd[slot, 1], preferred_element_type=F32)
        )

    gather(rg, sr_sem, rr_sem, backward, lambda: None)

    run = min(RUN, Z)
    runs = ring // run
    own_run, position = place // run, place % run
    for hh in range(H):
        csend[hh] = cacc[:, hh * half:(hh + 1) * half].astype(BF16)
    coords[0, own_rows] = csend[h]

    def place_peer(there):
        return {"dof": (there % Z) * X + x, "azi": ((there // Z) * Y + y) * 2 + core}

    def c_to_run(d):
        there = ((own_run + d) % runs) * run + position
        slot = d * run
        return remote(
            csend.at[there // Z], coords.at[slot, own_rows], scz_sem.at[slot], rcz_sem.at[slot],
            place_peer(there),
        )

    def c_in_run(d, n):
        slot = d * run + n
        return remote(
            coords.at[d * run, own_rows], coords.at[slot, own_rows], scz_sem.at[slot], rcz_sem.at[slot],
            place_peer(own_run * run + (position + n) % run),
        )

    def c_to_x(slot, q):
        return remote(
            coords.at[slot, own_rows], coords.at[slot, own_rows],
            scx_sem.at[slot, q - 1], rcx_sem.at[slot, q - 1], x_peer(q),
        )

    def c_from_x(slot, q):
        rows = pl.ds(pl.multiple_of(((x - q + X) % X) * fam, fam), fam)
        return remote(
            coords.at[slot, rows], coords.at[slot, rows],
            scx_sem.at[slot, q - 1], rcx_sem.at[slot, q - 1], x_peer(q),
        )

    def along_x(slot):
        for q in far_x:
            c_to_x(slot, q).start()

    def along_run(d):
        for n in range(1, run):
            c_in_run(d, n).start()

    def displace(n):
        k = n // run
        d = jnp.where(k % 2 == 1, (k + 1) // 2, (runs - k // 2) % runs)
        slot = d * run + n % run
        for q in range(1, X):
            c_from_x(slot, q).wait_recv()
        source = ((own_run - d + runs) % runs) * run + (position - n % run + run) % run
        block = coords[slot].astype(F32).T.astype(BF16)
        acc[source // Z] += lax.dot_general(
            block, s_v[(source % Z - z + Z) % Z], lanes, preferred_element_type=F32
        )

    def displace_all(low, high):
        if low < high:
            lax.fori_loop(low, high, lambda n, c: (displace(n), c)[1], 0)

    far = sorted(range(1, runs), key=lambda d: min(d, runs - d))
    for d in far[::-1]:
        c_to_run(d).start()
    along_run(0)
    along_x(0)
    acc[...] = jnp.zeros_like(acc)
    for n in range(1, run):
        c_in_run(0, n).wait_recv()
        along_x(n)
    done = 0
    for d in far:
        c_to_run(d).wait_recv()
        along_run(d)
        along_x(d * run)
        if d == far[-1]:
            displace_all(0, 1)
            done = 1
    for d in far:
        for n in range(1, run):
            c_in_run(d, n).wait_recv()
            along_x(d * run + n)
    displace_all(done, ring)

    out_v[...] = acc[...].astype(BF16).reshape(cases, own_t, depth)
    out_copy = pltpu.make_async_copy(out_v, out_hbm, o_sem)
    out_copy.start()

    def drain_x(o, carry):
        for r in range(1, X):
            x_copy(o, r).wait_send()
        return carry

    def drain_ring(r, carry):
        z_copy(r).wait_send()
        return carry

    def drain_coords(r, carry):
        for q in range(1, X):
            c_to_x(r, q).wait_send()
        return carry

    lax.fori_loop(0, Z, drain_x, 0)
    lax.fori_loop(1, ring, drain_ring, 0)
    lax.fori_loop(0, ring, drain_coords, 0)
    for d in far:
        c_to_run(d).wait_send()
    for d in range(runs):
        for n in range(1, run):
            c_in_run(d, n).wait_send()
    for k, n in sent_inverses:
        a_copy(k, n).wait_send()
    out_copy.wait()


def shards(dims, forcing, mode_shapes, inverses, harmonic_table):
    Z, X, H, Y = dims["Z"], dims["X"], dims["H"], dims["Y"]
    cases, own_t, depth = forcing.shape
    slots, _, _, fam, _ = inverses.shape
    ct = cases * own_t
    half = ct // H
    group = Y * 2
    length = H * group * own_t
    nh = harmonic_table.shape[0]
    ring = H * Z
    any_space = pl.BlockSpec(memory_space=pl.ANY)
    dma = pltpu.SemaphoreType.DMA
    xs = max(X - 1, 1)
    return pl.pallas_call(
        functools.partial(kernel, Z, X, H, Y),
        out_shape=jax.ShapeDtypeStruct(forcing.shape, BF16),
        in_specs=[any_space] * 4,
        out_specs=any_space,
        scratch_shapes=[
            pltpu.VMEM((cases, own_t, depth), BF16),
            pltpu.VMEM((Z, depth, X * fam), BF16),
            pltpu.VMEM((slots, 2, fam, fam), BF16),
            pltpu.VMEM((1, nh), jnp.int32),
            pltpu.VMEM((Z, X * fam, ct), F32),
            pltpu.VMEM((Z, X * fam, ct), BF16),
            pltpu.VMEM((Z, xs, fam, ct), BF16),
            pltpu.VMEM((Z, H, fam, half), BF16),
            pltpu.VMEM((ring, fam, half), BF16),
            pltpu.VMEM((H, fam, half), F32),
            pltpu.VMEM((length, ct), BF16),
            pltpu.VMEM((length, ct), BF16),
            pltpu.VMEM((length, ct), BF16),
            pltpu.VMEM((length, ct), BF16),
            pltpu.VMEM((group, 2, ct, ct), BF16),
            pltpu.VMEM((group, 2, ct, ct), BF16),
            pltpu.VMEM((slots * fam, 2 * fam), BF16),
            pltpu.VMEM((H, slots * fam, 2 * fam), BF16),
            pltpu.VMEM((group, fam, ct), BF16),
            pltpu.VMEM((group, fam, ct), BF16),
            pltpu.VMEM((fam, ct), F32),
            pltpu.VMEM((fam, ct), F32),
            pltpu.VMEM((H, fam, half), BF16),
            pltpu.VMEM((ring, X * fam, half), BF16),
            pltpu.VMEM((H, half, depth), F32),
            pltpu.VMEM((cases, own_t, depth), BF16),
            dma, dma((Z,)), dma, dma, dma, dma((H, INV_PIECES)), dma((H, INV_PIECES)),
            dma((Z, xs)), dma((Z, xs)), dma((ring,)), dma((ring,)),
            dma((group,)), dma((group,)), dma((group,)), dma((group,)),
            dma((ring,)), dma((ring,)), dma((ring, xs)), dma((ring, xs)),
        ],
        compiler_params=pltpu.CompilerParams(
            collective_id=0, has_side_effects=True, vmem_limit_bytes=60 * 1024 * 1024
        ),
        name="forced_response",
    )(
        forcing,
        mode_shapes,
        inverses.reshape(slots, 2, fam, fam),
        harmonic_table.reshape(1, nh),
    )


def solution(mesh, dims=DIMS):
    in_specs = (P(None, "azi", "dof"), P("dof", None), P("azi", "dof", None, None, None), P())
    out_specs = P(None, "azi", "dof")
    return jax.shard_map(
        functools.partial(shards, dims), mesh=mesh, in_specs=in_specs, out_specs=out_specs, check_vma=False
    )
```
